128 devices in a mesh: dp: 8 (over z, y_hi), tensor: 16 (over y_lo, x, core).
Axes of the slice: x: 4, y: 4 (y_hi: 2, y_lo: 2; y = y_hi * 2 + y_lo), z: 4, core: 2. Of those that a mesh axis runs over, the one named last changes fastest.
Arguments:
- hidden_act: bfloat16 [4096, 18432], P('dp', 'tensor'), may hold values from -0.09375 to 0.09375
- out_grad: bfloat16 [4096, 4608], P('dp', 'tensor'), may hold values from -6 to 6
- down_weight: bfloat16 [18432, 4608], P(None, 'tensor'), may hold values from -0.125 to 0.125
Outputs:
- hidden_grad: bfloat16 [18432, 4096], P('tensor', 'dp')
- weight_grad: float32 [18432, 4608], P(('tensor', 'dp'))
The draws below stay inside these ranges and needn't reach their ends.
All inputs are finite; a program needn't handle non-finite values.
Results may differ from the reference program's by a relative error of at most 0.022.
Values may be sent and summed in bfloat16 or wider, within the bound.
A program may use at most 192 MiB of HBM per device.

```python
import jax
import jax.numpy as jnp
from jax import lax

D = 4608
FF = 18432
TOK_DEV = 512
TOKENS = 4096
N_DP = 8
N_TENSOR = 16


def with_spikes(entries, stream_key, source, target, shards_of, factor):
    owner, partner = [(jnp.arange(entries.shape[position]) // (entries.shape[position] // shards_of)).reshape([-1 if axis == position else 1 for axis in range(entries.ndim)]) for position in (source, target)]
    chosen = jax.random.permutation(stream_key, shards_of)[partner]
    strong = (owner == chosen) | (owner == (partner + shards_of // 2) % shards_of)
    return jnp.where(strong, factor * entries, entries)


def steps_of(key, dims, split, low, largest):
    def one(dim, blocks):
        steps = jax.random.uniform(jax.random.fold_in(jax.random.fold_in(key, 6), dim), (blocks,), jnp.float32, low / len(split), largest / len(split))
        return jnp.repeat(jnp.exp(steps), dims[dim] // blocks).reshape((-1,) + (1,) * (len(dims) - dim - 1))

    loudness = one(*split[0])
    for cut in split[1:]:
        loudness = loudness * one(*cut)
    return loudness


def scatter_about(stream_key, extent, width, reach, split=(), kind=jnp.bfloat16):
    drawn = width * jax.random.normal(stream_key, extent, jnp.float32)
    if split:
        drawn = drawn * steps_of(stream_key, extent, split, -0.22, 0.18)
    return jnp.clip(drawn, -reach, reach).astype(kind)


def heavy_noise(key, extent, spread, bound, cuts, heavy, dtype=jnp.bfloat16):
    result = spread * jax.random.normal(key, extent, jnp.float32)
    if cuts:
        result = result * steps_of(key, extent, cuts, -0.22, 0.18)
    return jnp.clip(with_spikes(result, jax.random.fold_in(key, 3), *heavy), -bound, bound).astype(dtype)


def setup_inputs(seed: int = 0) -> dict:
    key_list = jax.random.split(jax.random.key(seed), 4)
    return {
        "hidden_act": heavy_noise(key_list[0], (TOKENS, FF), (1.0 / (TOKENS ** 0.5)), 0.09375, ((0, 8), (1, 16)), (0, 1, 16, 2.0)),
        "out_grad": scatter_about(key_list[1], (TOKENS, D), 1.0, 6.0, ((0, 8), (1, 16))),
        "down_weight": heavy_noise(key_list[2], (FF, D), D ** -0.5, 0.125, ((1, 16),), (1, 0, 16, 2.0)),
    }


def reference(hidden_act, out_grad, down_weight):
    group = D // N_TENSOR
    total = jnp.zeros((FF, TOKENS), jnp.float32)
    for g in range(N_TENSOR):
        part = lax.dot_general(down_weight[:, g * group:(g + 1) * group], out_grad[:, g * group:(g + 1) * group], (((1,), (1,)), ((), ())), preferred_element_type=jnp.float32)
        part = lax.optimization_barrier(part.astype(jnp.bfloat16))
        total = total + part.astype(jnp.float32)
    hidden_grad = total.astype(jnp.bfloat16)
    weight_grad = jnp.zeros((FF, D), jnp.float32)
    for r in range(N_DP):
        rows_h = hidden_act[r * TOK_DEV:(r + 1) * TOK_DEV]
        rows_g = out_grad[r * TOK_DEV:(r + 1) * TOK_DEV]
        part = lax.dot_general(rows_h, rows_g, (((0,), (0,)), ((), ())), preferred_element_type=jnp.float32)
        weight_grad = weight_grad + part
    return hidden_grad, weight_grad
```

```python
import functools

import jax
import jax.numpy as jnp
from jax import lax
from jax.experimental import pallas as pl
from jax.experimental.pallas import tpu as pltpu
from jax.sharding import PartitionSpec as P

MESH = pl.DeviceIdType.MESH
BF = jnp.bfloat16
F32 = jnp.float32
DB = 288
HB = 144
TB = 512
FB = 1152
ROW = 4 * DB
PARTS = ((0, 640), (640, 512))
TILE = 384

W_MOVES = [(1, 0, 0, DB), (-1, 0, 0, DB), (2, 0, 0, DB)]
for _dx in (0, 1, -1, 2):
    W_MOVES += [(_dx, 1, 0, HB), (_dx, -1, HB, HB)]
N_W = len(W_MOVES)
PARTNERS = [(1, 0, 0, 0), (-1, 0, 0, 0), (2, 0, 0, 0), (0, 2, 0, 0), (0, 0, 1, 0), (0, 0, -1, 0), (0, 0, 0, 1), (0, 2, 0, 1)]
PARTNERS += [(dx, dy, 0, 0) for dx in (0, 1, -1, 2) for dy in (1, -1)]
NT = (((1,), (1,)), ((), ()))


def kernel(a_ref, g_ref, w_ref, hg_ref, wg_ref, G, Wb, Wt, T, AT, SB, FW, RV, H, OWN, XS, XR, XB, YB, R, ss, rs, ws, wr, ls):
    t = lax.axis_index("tensor")
    r = lax.axis_index("dp")
    c = lax.rem(t, 2)
    x = lax.rem(t // 2, 4)
    l = t // 8
    h = lax.rem(r, 2)
    z = r // 2
    y = 2 * h + l

    def dev(dx, dy, dz, dc):
        X = lax.rem(x + (dx + 4), 4)
        Y = lax.rem(y + (dy + 4), 4)
        Z = lax.rem(z + (dz + 4), 4)
        C = lax.rem(c + dc, 2)
        return (Z * 2 + Y // 2, lax.rem(Y, 2) * 8 + X * 2 + C)

    def rcopy(k, src, dst, offset):
        return pltpu.make_async_remote_copy(
            src_ref=src, dst_ref=dst, send_sem=ss.at[k], recv_sem=rs.at[k], device_id=dev(*offset), device_id_type=MESH
        )

    started = []

    def go(k, src, dst, offset):
        cp = rcopy(k, src, dst, offset)
        cp.start()
        started.append(cp)
        return cp

    barrier = pltpu.get_barrier_semaphore()
    for offset in PARTNERS:
        pl.semaphore_signal(barrier, inc=1, device_id=dev(*offset), device_id_type=MESH)
    pl.semaphore_wait(barrier, len(PARTNERS))

    def slot(rep, ll, xx, lo=0, n=DB):
        return G.at[rep, pl.ds(pl.multiple_of((ll * 4 + xx) * DB + lo, 16), n), :]

    xm = lax.rem(x + 3, 4)
    xp = lax.rem(x + 1, 4)
    o = 1 - h
    k0 = go(0, g_ref, slot(h, l, x), (1, 0, 0, 0))
    k1 = go(1, g_ref, slot(h, l, x), (-1, 0, 0, 0))
    k2 = go(2, g_ref, slot(h, l, x), (0, 2, 0, 0))
    fo = pl.multiple_of((l * 8 + x * 2 + h) * FB, 128)
    own_w = pltpu.make_async_copy(
        w_ref.at[:, pl.ds(fo, FB)], Wb.at[pl.ds(pl.multiple_of((l * 4 + x) * DB, 16), DB), :], ls.at[0]
    )
    own_w.start()
    G[h, pl.ds(pl.multiple_of((l * 4 + x) * DB, 16), DB), :] = g_ref[...]

    T[...] = a_ref[...].T.reshape(4, 2, HB, TB)
    k11 = go(11, T.at[:, o], AT.at[h, :, c], (0, 2, 0, 0))
    AT[h, :, c] = T[:, h]
    k12 = go(12, AT.at[h, :, c], AT.at[h, :, c], (0, 0, 0, 1))

    k0.wait_recv()
    k3 = go(3, slot(h, l, xm, 0, HB), slot(h, l, xm, 0, HB), (1, 0, 0, 0))
    k1.wait_recv()
    k4 = go(4, slot(h, l, xp, HB, HB), slot(h, l, xp, HB, HB), (-1, 0, 0, 0))
    k2.wait_recv()
    k5 = go(5, slot(o, l, x), slot(o, l, x), (1, 0, 0, 0))
    k6 = go(6, slot(o, l, x), slot(o, l, x), (-1, 0, 0, 0))
    k3.wait_recv()
    k4.wait_recv()
    own_row = G.at[h, pl.ds(pl.multiple_of(l * ROW, 16), ROW), :]
    k7 = go(7, own_row, own_row, (0, 1, 0, 0))
    k8 = go(8, own_row, own_row, (0, -1, 0, 0))
    k5.wait_recv()
    k9 = go(9, slot(o, l, xm, 0, HB), slot(o, l, xm, 0, HB), (1, 0, 0, 0))
    k6.wait_recv()
    k10 = go(10, slot(o, l, xp, HB, HB), slot(o, l, xp, HB, HB), (-1, 0, 0, 0))

    w_copies = [[], []]

    def send_weights(p):
        lo, n = PARTS[p]
        for i, (dx, dy, first, rows) in enumerate(W_MOVES):
            X = lax.rem(x + (dx + 4), 4)
            Y = lax.rem(y + (dy + 4), 4)
            col = pl.multiple_of((lax.rem(Y, 2) * 8 + X * 2 + Y // 2) * FB + lo, 128)
            cp = pltpu.make_async_remote_copy(
                src_ref=w_ref.at[pl.ds(first, rows), pl.ds(col, n)],
                dst_ref=Wb.at[pl.ds(pl.multiple_of((l * 4 + x) * DB + first, 16), rows), pl.ds(lo, n)],
                send_sem=ws.at[p, i],
                recv_sem=wr.at[p, i],
                device_id=dev(dx, dy, 0, 0),
                device_id_type=MESH,
            )
            cp.start()
            w_copies[p].append(cp)

    send_weights(0)

    k11.wait_recv()
    k13 = go(13, AT.at[o, :, c], AT.at[o, :, c], (0, 0, 0, 1))
    k12.wait_recv()
    k13.wait_recv()
    k9.wait_recv()
    k10.wait_recv()

    def tile(zz, ll, n):
        rows = pl.ds(pl.multiple_of(ll * ROW + n * TILE, 16), TILE)
        acc = lax.dot_general(AT[0, zz].reshape(2 * HB, TB), G[0, rows, :], NT, preferred_element_type=F32)
        acc += lax.dot_general(AT[1, zz].reshape(2 * HB, TB), G[1, rows, :], NT, preferred_element_type=F32)
        return acc

    def cols(n):
        return pl.ds(pl.multiple_of(n * TILE, 128), TILE)

    zp = lax.rem(z + 1, 4)
    zm = lax.rem(z + 3, 4)
    zo = lax.rem(z + 2, 4)

    def chunk_send(j):
        ll = l if j == 0 else 1 - l
        base = 14 + 8 * j

        @pl.loop(0, ROW // TILE)
        def _(n):
            SB[j, 0, :, :, cols(n)] = tile(zo, ll, n).reshape(2, HB, TILE).astype(BF)

        up = go(base + 0, SB.at[j, 0, 0], FW.at[j, 0], (0, 0, 1, 0))
        down = go(base + 1, SB.at[j, 0, 1], FW.at[j, 1], (0, 0, -1, 0))

        @pl.loop(0, ROW // TILE)
        def _(n):
            part = tile(zp, ll, n).reshape(2, HB, TILE)
            SB[j, 1, 1, :, cols(n)] = part[1].astype(BF)
            H[0, :, cols(n)] = part[0]

        c0 = go(base + 2, SB.at[j, 1, 1], RV.at[j, 0, 1], (0, 0, 1, 0))

        @pl.loop(0, ROW // TILE)
        def _(n):
            part = tile(zm, ll, n).reshape(2, HB, TILE)
            SB[j, 2, 0, :, cols(n)] = part[0].astype(BF)
            H[1, :, cols(n)] = part[1]

        c1 = go(base + 3, SB.at[j, 2, 0], RV.at[j, 1, 0], (0, 0, -1, 0))
        up.wait_recv()
        SB[j, 1, 0] = (H[0] + FW[j, 0].astype(F32)).astype(BF)
        c2 = go(base + 4, SB.at[j, 1, 0], RV.at[j, 0, 0], (0, 0, 1, 0))
        down.wait_recv()
        SB[j, 2, 1] = (H[1] + FW[j, 1].astype(F32)).astype(BF)
        c3 = go(base + 5, SB.at[j, 2, 1], RV.at[j, 1, 1], (0, 0, -1, 0))
        return c0, c1, c2, c3

    def chunk_own(j):
        ll = l if j == 0 else 1 - l

        @pl.loop(0, ROW // TILE)
        def _(n):
            OWN[j, :, :, cols(n)] = tile(z, ll, n).reshape(2, HB, TILE)

    def chunk_end(j, copies):
        for cp in copies:
            cp.wait_recv()
        XS[j] = (OWN[j, 1 - c] + RV[j, 0, 1 - c].astype(F32) + RV[j, 1, 1 - c].astype(F32)).astype(BF)
        swap = go(20 + 8 * j, XS.at[j], XR.at[j], (0, 0, 0, 1))
        OWN[j, c] = OWN[j, c] + RV[j, 0, c].astype(F32) + RV[j, 1, c].astype(F32)
        return swap

    def chunk_out(j, swap):
        ll = l if j == 0 else 1 - l
        swap.wait_recv()
        mine = OWN[j, c]
        other = XR[j].astype(F32)
        even = jnp.where(c == 0, mine, other)
        odd = jnp.where(c == 0, other, mine)
        pieces = []
        for xx in range(4):
            pieces += [even[:, xx * DB:(xx + 1) * DB], odd[:, xx * DB:(xx + 1) * DB]]
        wg_ref[:, pl.ds(pl.multiple_of(ll * 2 * ROW, 128), 2 * ROW)] = jnp.concatenate(pieces, axis=1)

    def hidden(p):
        lo, n = PARTS[p]
        if p == 0:
            own_w.wait()
        for cp in w_copies[p]:
            cp.wait_recv()

        @pl.loop(0, 2 * ROW // 256)
        def _(k):
            rows = pl.ds(pl.multiple_of(k * 256, 256), 256)
            Wt[pl.ds(0, n), rows] = Wb[rows, pl.ds(lo, n)].T

        def product(rep, q):
            return jnp.dot(Wt[pl.ds(0, n), :], G[rep, :, pl.ds(pl.multiple_of(q * 256, 256), 256)], preferred_element_type=F32)

        @pl.loop(0, 2)
        def _(q):
            XB[p, pl.ds(0, n), pl.ds(pl.multiple_of(q * 256, 256), 256)] = product(1 - c, q).astype(BF)

        half = rcopy(30 + 2 * p, XB.at[p, pl.ds(0, n)], YB.at[p, pl.ds(0, n)], (0, 0, 0, 1))
        half.start()

        @pl.loop(0, 2)
        def _(q):
            H2 = pl.ds(pl.multiple_of(q * 256, 256), 256)
            R[p, pl.ds(0, n), H2] = product(c, q)

        half.wait_recv()
        XB2 = (R[p, pl.ds(0, n), :] + YB[p, pl.ds(0, n), :].astype(F32)).astype(BF)
        half.wait_send()
        XB[p, pl.ds(0, n), :] = XB2
        final = rcopy(31 + 2 * p, XB.at[p, pl.ds(0, n)], hg_ref.at[pl.ds(lo, n)], (0, 2, 0, 1))

        @pl.when(c != h)
        def _():
            final.start()

        @pl.when(c == h)
        def _():
            hg_ref[pl.ds(lo, n), :] = XB2

        return final

    first = chunk_send(0)
    chunk_own(0)
    k7.wait_recv()
    k8.wait_recv()
    send_weights(1)
    second = chunk_send(1)
    chunk_own(1)
    swap0 = chunk_end(0, first)
    f0 = hidden(0)
    chunk_out(0, swap0)
    swap1 = chunk_end(1, second)
    f1 = hidden(1)
    chunk_out(1, swap1)

    @pl.when(c != h)
    def _():
        f0.wait()
        f1.wait()

    for cp in started:
        cp.wait_send()
    for p in range(2):
        for cp in w_copies[p]:
            cp.wait_send()


def per_device(hidden_act, out_grad, down_weight):
    scratch = [
        pltpu.VMEM((2, 2 * ROW, TB), BF),
        pltpu.VMEM((2 * ROW, FB), BF),
        pltpu.VMEM((640, 2 * ROW), BF),
        pltpu.VMEM((4, 2, HB, TB), BF),
        pltpu.VMEM((2, 4, 2, HB, TB), BF),
        pltpu.VMEM((2, 3, 2, HB, ROW), BF),
        pltpu.VMEM((2, 2, HB, ROW), BF),
        pltpu.VMEM((2, 2, 2, HB, ROW), BF),
        pltpu.VMEM((2, HB, ROW), F32),
        pltpu.VMEM((2, 2, HB, ROW), F32),
        pltpu.VMEM((2, HB, ROW), BF),
        pltpu.VMEM((2, HB, ROW), BF),
        pltpu.VMEM((2, 640, TB), BF),
        pltpu.VMEM((2, 640, TB), BF),
        pltpu.VMEM((2, 640, TB), F32),
        pltpu.SemaphoreType.DMA((34,)),
        pltpu.SemaphoreType.DMA((34,)),
        pltpu.SemaphoreType.DMA((2, N_W)),
        pltpu.SemaphoreType.DMA((2, N_W)),
        pltpu.SemaphoreType.DMA((1,)),
    ]
    vmem = pl.BlockSpec(memory_space=pltpu.VMEM)
    return pl.pallas_call(
        kernel,
        out_shape=(jax.ShapeDtypeStruct((FB, TB), BF), jax.ShapeDtypeStruct((HB, 16 * DB), F32)),
        in_specs=[vmem, vmem, pl.BlockSpec(memory_space=pl.ANY)],
        out_specs=(vmem, vmem),
        scratch_shapes=scratch,
        compiler_params=pltpu.CompilerParams(collective_id=0, has_side_effects=True, vmem_limit_bytes=60 * 2**20),
        cost_estimate=pl.CostEstimate(flops=10_900_000_000, bytes_accessed=20_000_000, transcendentals=0),
    )(hidden_act, out_grad.T, down_weight.T)


def solution(mesh):
    return jax.shard_map(
        per_device,
        mesh=mesh,
        in_specs=(P("dp", "tensor"), P("dp", "tensor"), P(None, "tensor")),
        out_specs=(P("tensor", "dp"), P(("tensor", "dp"), None)),
        check_vma=False,
    )
```

```python
import functools

import jax
import jax.numpy as jnp
from jax import lax
from jax.experimental import pallas as pl
from jax.experimental.pallas import tpu as pltpu
from jax.sharding import PartitionSpec as P

MESH = pl.DeviceIdType.MESH
BF = jnp.bfloat16
F32 = jnp.float32
DB = 288
HB = 144
TB = 512
FB = 1152
ROW = 4 * DB
PARTS = ((0, 640), (640, 512))
TILE = 384

W_MOVES = [(1, 0, 0, DB), (-1, 0, 0, DB), (2, 0, 0, DB)]
for _dx in (0, 1, -1, 2):
    W_MOVES += [(_dx, 1, 0, HB), (_dx, -1, HB, HB)]
N_W = len(W_MOVES)
PARTNERS = [(1, 0, 0, 0), (-1, 0, 0, 0), (2, 0, 0, 0), (0, 2, 0, 0), (0, 0, 1, 0), (0, 0, -1, 0), (0, 0, 0, 1), (0, 2, 0, 1)]
PARTNERS += [(dx, dy, 0, 0) for dx in (0, 1, -1, 2) for dy in (1, -1)]
NT = (((1,), (1,)), ((), ()))


def kernel(a_hbm, g_hbm, w_ref, hg_ref, wg_ref, a_ref, g_ref, G, Wb, Wt, T, AT, SB, FW, RV, H, OWN, XS, XR, XB, YB, R, ss, rs, ws, wr, ls):
    t = lax.axis_index("tensor")
    r = lax.axis_index("dp")
    c = lax.rem(t, 2)
    x = lax.rem(t // 2, 4)
    l = t // 8
    h = lax.rem(r, 2)
    z = r // 2
    y = 2 * h + l

    def dev(dx, dy, dz, dc):
        X = lax.rem(x + (dx + 4), 4)
        Y = lax.rem(y + (dy + 4), 4)
        Z = lax.rem(z + (dz + 4), 4)
        C = lax.rem(c + dc, 2)
        return (Z * 2 + Y // 2, lax.rem(Y, 2) * 8 + X * 2 + C)

    def rcopy(k, src, dst, offset):
        return pltpu.make_async_remote_copy(
            src_ref=src, dst_ref=dst, send_sem=ss.at[k], recv_sem=rs.at[k], device_id=dev(*offset), device_id_type=MESH
        )

    started = []

    def go(k, src, dst, offset):
        cp = rcopy(k, src, dst, offset)
        cp.start()
        started.append(cp)
        return cp

    load_g = pltpu.make_async_copy(g_hbm, g_ref, ls.at[1])
    load_g.start()
    load_a = pltpu.make_async_copy(a_hbm, a_ref, ls.at[2])
    load_a.start()
    barrier = pltpu.get_barrier_semaphore()
    for offset in PARTNERS:
        pl.semaphore_signal(barrier, inc=1, device_id=dev(*offset), device_id_type=MESH)
    pl.semaphore_wait(barrier, len(PARTNERS))

    load_g.wait()
    def slot(rep, ll, xx, lo=0, n=DB):
        return G.at[rep, pl.ds(pl.multiple_of((ll * 4 + xx) * DB + lo, 16), n), :]

    xm = lax.rem(x + 3, 4)
    xp = lax.rem(x + 1, 4)
    o = 1 - h
    k0 = go(0, g_ref, slot(h, l, x), (1, 0, 0, 0))
    k1 = go(1, g_ref, slot(h, l, x), (-1, 0, 0, 0))
    k2 = go(2, g_ref, slot(h, l, x), (0, 2, 0, 0))
    fo = pl.multiple_of((l * 8 + x * 2 + h) * FB, 128)
    own_w = pltpu.make_async_copy(
        w_ref.at[:, pl.ds(fo, FB)], Wb.at[pl.ds(pl.multiple_of((l * 4 + x) * DB, 16), DB), :], ls.at[0]
    )
    own_w.start()
    G[h, pl.ds(pl.multiple_of((l * 4 + x) * DB, 16), DB), :] = g_ref[...]

    load_a.wait()
    T[...] = a_ref[...].T.reshape(4, 2, HB, TB)
    k11 = go(11, T.at[:, o], AT.at[h, :, c], (0, 2, 0, 0))
    AT[h, :, c] = T[:, h]
    k12 = go(12, AT.at[h, :, c], AT.at[h, :, c], (0, 0, 0, 1))

    k0.wait_recv()
    k3 = go(3, slot(h, l, xm, 0, HB), slot(h, l, xm, 0, HB), (1, 0, 0, 0))
    k1.wait_recv()
    k4 = go(4, slot(h, l, xp, HB, HB), slot(h, l, xp, HB, HB), (-1, 0, 0, 0))
    k2.wait_recv()
    k5 = go(5, slot(o, l, x), slot(o, l, x), (1, 0, 0, 0))
    k6 = go(6, slot(o, l, x), slot(o, l, x), (-1, 0, 0, 0))
    k3.wait_recv()
    k4.wait_recv()
    own_row = G.at[h, pl.ds(pl.multiple_of(l * ROW, 16), ROW), :]
    k7 = go(7, own_row, own_row, (0, 1, 0, 0))
    k8 = go(8, own_row, own_row, (0, -1, 0, 0))
    k5.wait_recv()
    k9 = go(9, slot(o, l, xm, 0, HB), slot(o, l, xm, 0, HB), (1, 0, 0, 0))
    k6.wait_recv()
    k10 = go(10, slot(o, l, xp, HB, HB), slot(o, l, xp, HB, HB), (-1, 0, 0, 0))

    w_copies = [[], []]

    def send_weights(p):
        lo, n = PARTS[p]
        for i, (dx, dy, first, rows) in enumerate(W_MOVES):
            X = lax.rem(x + (dx + 4), 4)
            Y = lax.rem(y + (dy + 4), 4)
            col = pl.multiple_of((lax.rem(Y, 2) * 8 + X * 2 + Y // 2) * FB + lo, 128)
            cp = pltpu.make_async_remote_copy(
                src_ref=w_ref.at[pl.ds(first, rows), pl.ds(col, n)],
                dst_ref=Wb.at[pl.ds(pl.multiple_of((l * 4 + x) * DB + first, 16), rows), pl.ds(lo, n)],
                send_sem=ws.at[p, i],
                recv_sem=wr.at[p, i],
                device_id=dev(dx, dy, 0, 0),
                device_id_type=MESH,
            )
            cp.start()
            w_copies[p].append(cp)

    send_weights(0)

    k11.wait_recv()
    k13 = go(13, AT.at[o, :, c], AT.at[o, :, c], (0, 0, 0, 1))
    k12.wait_recv()
    k13.wait_recv()
    k9.wait_recv()
    k10.wait_recv()

    def tile(zz, ll, n):
        rows = pl.ds(pl.multiple_of(ll * ROW + n * TILE, 16), TILE)
        acc = lax.dot_general(AT[0, zz].reshape(2 * HB, TB), G[0, rows, :], NT, preferred_element_type=F32)
        acc += lax.dot_general(AT[1, zz].reshape(2 * HB, TB), G[1, rows, :], NT, preferred_element_type=F32)
        return acc

    def cols(n):
        return pl.ds(pl.multiple_of(n * TILE, 128), TILE)

    zp = lax.rem(z + 1, 4)
    zm = lax.rem(z + 3, 4)
    zo = lax.rem(z + 2, 4)

    def chunk_send(j):
        ll = l if j == 0 else 1 - l
        base = 14 + 8 * j

        @pl.loop(0, ROW // TILE)
        def _(n):
            SB[j, 0, :, :, cols(n)] = tile(zo, ll, n).reshape(2, HB, TILE).astype(BF)

        up = go(base + 0, SB.at[j, 0, 0], FW.at[j, 0], (0, 0, 1, 0))
        down = go(base + 1, SB.at[j, 0, 1], FW.at[j, 1], (0, 0, -1, 0))

        @pl.loop(0, ROW // TILE)
        def _(n):
            part = tile(zp, ll, n).reshape(2, HB, TILE)
            SB[j, 1, 1, :, cols(n)] = part[1].astype(BF)
            H[0, :, cols(n)] = part[0]

        c0 = go(base + 2, SB.at[j, 1, 1], RV.at[j, 0, 1], (0, 0, 1, 0))

        @pl.loop(0, ROW // TILE)
        def _(n):
            part = tile(zm, ll, n).reshape(2, HB, TILE)
            SB[j, 2, 0, :, cols(n)] = part[0].astype(BF)
            H[1, :, cols(n)] = part[1]

        c1 = go(base + 3, SB.at[j, 2, 0], RV.at[j, 1, 0], (0, 0, -1, 0))
        up.wait_recv()
        SB[j, 1, 0] = (H[0] + FW[j, 0].astype(F32)).astype(BF)
        c2 = go(base + 4, SB.at[j, 1, 0], RV.at[j, 0, 0], (0, 0, 1, 0))
        down.wait_recv()
        SB[j, 2, 1] = (H[1] + FW[j, 1].astype(F32)).astype(BF)
        c3 = go(base + 5, SB.at[j, 2, 1], RV.at[j, 1, 1], (0, 0, -1, 0))
        return c0, c1, c2, c3

    def chunk_own(j):
        ll = l if j == 0 else 1 - l

        @pl.loop(0, ROW // TILE)
        def _(n):
            OWN[j, :, :, cols(n)] = tile(z, ll, n).reshape(2, HB, TILE)

    def chunk_end(j, copies):
        for cp in copies:
            cp.wait_recv()
        XS[j] = (OWN[j, 1 - c] + RV[j, 0, 1 - c].astype(F32) + RV[j, 1, 1 - c].astype(F32)).astype(BF)
        swap = go(20 + 8 * j, XS.at[j], XR.at[j], (0, 0, 0, 1))
        OWN[j, c] = OWN[j, c] + RV[j, 0, c].astype(F32) + RV[j, 1, c].astype(F32)
        return swap

    def chunk_out(j, swap):
        ll = l if j == 0 else 1 - l
        swap.wait_recv()
        mine = OWN[j, c]
        other = XR[j].astype(F32)
        even = jnp.where(c == 0, mine, other)
        odd = jnp.where(c == 0, other, mine)
        pieces = []
        for xx in range(4):
            pieces += [even[:, xx * DB:(xx + 1) * DB], odd[:, xx * DB:(xx + 1) * DB]]
        wg_ref[:, pl.ds(pl.multiple_of(ll * 2 * ROW, 128), 2 * ROW)] = jnp.concatenate(pieces, axis=1)

    def hidden(p):
        lo, n = PARTS[p]
        if p == 0:
            own_w.wait()
        for cp in w_copies[p]:
            cp.wait_recv()

        @pl.loop(0, 2 * ROW // 256)
        def _(k):
            rows = pl.ds(pl.multiple_of(k * 256, 256), 256)
            Wt[pl.ds(0, n), rows] = Wb[rows, pl.ds(lo, n)].T

        def product(rep, q):
            return jnp.dot(Wt[pl.ds(0, n), :], G[rep, :, pl.ds(pl.multiple_of(q * 256, 256), 256)], preferred_element_type=F32)

        @pl.loop(0, 2)
        def _(q):
            XB[p, pl.ds(0, n), pl.ds(pl.multiple_of(q * 256, 256), 256)] = product(1 - c, q).astype(BF)

        half = rcopy(30 + 2 * p, XB.at[p, pl.ds(0, n)], YB.at[p, pl.ds(0, n)], (0, 0, 0, 1))
        half.start()

        @pl.loop(0, 2)
        def _(q):
            H2 = pl.ds(pl.multiple_of(q * 256, 256), 256)
            R[p, pl.ds(0, n), H2] = product(c, q)

        half.wait_recv()
        XB2 = (R[p, pl.ds(0, n), :] + YB[p, pl.ds(0, n), :].astype(F32)).astype(BF)
        half.wait_send()
        XB[p, pl.ds(0, n), :] = XB2
        final = rcopy(31 + 2 * p, XB.at[p, pl.ds(0, n)], hg_ref.at[pl.ds(lo, n)], (0, 2, 0, 1))

        @pl.when(c != h)
        def _():
            final.start()

        @pl.when(c == h)
        def _():
            hg_ref[pl.ds(lo, n), :] = XB2

        return final

    first = chunk_send(0)
    chunk_own(0)
    k7.wait_recv()
    k8.wait_recv()
    send_weights(1)
    second = chunk_send(1)
    chunk_own(1)
    swap0 = chunk_end(0, first)
    f0 = hidden(0)
    chunk_out(0, swap0)
    swap1 = chunk_end(1, second)
    f1 = hidden(1)
    chunk_out(1, swap1)

    @pl.when(c != h)
    def _():
        f0.wait()
        f1.wait()

    for cp in started:
        cp.wait_send()
    for p in range(2):
        for cp in w_copies[p]:
            cp.wait_send()


def per_device(hidden_act, out_grad, down_weight):
    scratch = [
        pltpu.VMEM((TB, FB), BF),
        pltpu.VMEM((DB, TB), BF),
        pltpu.VMEM((2, 2 * ROW, TB), BF),
        pltpu.VMEM((2 * ROW, FB), BF),
        pltpu.VMEM((640, 2 * ROW), BF),
        pltpu.VMEM((4, 2, HB, TB), BF),
        pltpu.VMEM((2, 4, 2, HB, TB), BF),
        pltpu.VMEM((2, 3, 2, HB, ROW), BF),
        pltpu.VMEM((2, 2, HB, ROW), BF),
        pltpu.VMEM((2, 2, 2, HB, ROW), BF),
        pltpu.VMEM((2, HB, ROW), F32),
        pltpu.VMEM((2, 2, HB, ROW), F32),
        pltpu.VMEM((2, HB, ROW), BF),
        pltpu.VMEM((2, HB, ROW), BF),
        pltpu.VMEM((2, 640, TB), BF),
        pltpu.VMEM((2, 640, TB), BF),
        pltpu.VMEM((2, 640, TB), F32),
        pltpu.SemaphoreType.DMA((34,)),
        pltpu.SemaphoreType.DMA((34,)),
        pltpu.SemaphoreType.DMA((2, N_W)),
        pltpu.SemaphoreType.DMA((2, N_W)),
        pltpu.SemaphoreType.DMA((3,)),
    ]
    vmem = pl.BlockSpec(memory_space=pltpu.VMEM)
    held = pl.pallas_call(
        kernel,
        out_shape=(pltpu.VMEM((FB, TB), BF), pltpu.VMEM((HB, 16 * DB), F32)),
        in_specs=[pl.BlockSpec(memory_space=pl.ANY)] * 3,
        out_specs=(vmem, vmem),
        scratch_shapes=scratch,
        compiler_params=pltpu.CompilerParams(collective_id=0, has_side_effects=True, vmem_limit_bytes=63_000_000),
        cost_estimate=pl.CostEstimate(flops=10_900_000_000, bytes_accessed=20_000_000, transcendentals=0),
    )(hidden_act, out_grad.T, down_weight.T)
    return held


def solution(mesh):
    return jax.shard_map(
        per_device,
        mesh=mesh,
        in_specs=(P("dp", "tensor"), P("dp", "tensor"), P(None, "tensor")),
        out_specs=(P("tensor", "dp"), P(("tensor", "dp"), None)),
        check_vma=False,
    )
```

```python
import functools

import jax
import jax.numpy as jnp
from jax import lax
from jax.experimental import pallas as pl
from jax.experimental.pallas import tpu as pltpu
from jax.sharding import PartitionSpec as P

MESH = pl.DeviceIdType.MESH
BF = jnp.bfloat16
F32 = jnp.float32
DB = 288
HB = 144
TB = 512
FB = 1152
ROW = 4 * DB
PART = 384
N_PARTS = FB // PART
TILE = 384

NEAR = [(1, 0, 0, DB), (-1, 0, 0, DB), (2, 0, 0, DB)]
FAR = []
for _dx in (0, 1, -1, 2):
    FAR += [(_dx, 1, 0, HB), (_dx, -1, HB, HB)]
N_SEM = 80
PARTNERS = [(1, 0, 0, 0), (-1, 0, 0, 0), (2, 0, 0, 0), (0, 2, 0, 0), (0, 0, 1, 0), (0, 0, -1, 0), (0, 0, 0, 1), (0, 2, 0, 1)]
PARTNERS += [(dx, dy, 0, 0) for dx in (0, 1, -1, 2) for dy in (1, -1)]
NT = (((1,), (1,)), ((), ()))


def kernel(a_hbm, g_hbm, w_ref, hg_ref, wg_ref, a_ref, g_ref, G, Wb, Wt, T, AT, SB, FW, RV, H, OWN, XS, XR, XB, YB, XF, R, ss, rs, ls):
    t = lax.axis_index("tensor")
    r = lax.axis_index("dp")
    c = lax.rem(t, 2)
    x = lax.rem(t // 2, 4)
    l = t // 8
    h = lax.rem(r, 2)
    z = r // 2
    y = 2 * h + l

    def dev(dx, dy, dz, dc):
        X = lax.rem(x + (dx + 4), 4)
        Y = lax.rem(y + (dy + 4), 4)
        Z = lax.rem(z + (dz + 4), 4)
        C = lax.rem(c + dc, 2)
        return (Z * 2 + Y // 2, lax.rem(Y, 2) * 8 + X * 2 + C)

    count = [0]
    started = []

    def prepare(src, dst, offset):
        k = count[0]
        count[0] += 1
        return pltpu.make_async_remote_copy(
            src_ref=src, dst_ref=dst, send_sem=ss.at[k], recv_sem=rs.at[k], device_id=dev(*offset), device_id_type=MESH
        )

    def go(src, dst, offset):
        cp = prepare(src, dst, offset)
        cp.start()
        started.append(cp)
        return cp

    def same(ref, offset):
        return go(ref, ref, offset)

    load_g = pltpu.make_async_copy(g_hbm, g_ref, ls.at[1])
    load_g.start()
    load_a = pltpu.make_async_copy(a_hbm, a_ref, ls.at[2])
    load_a.start()
    barrier = pltpu.get_barrier_semaphore()
    for offset in PARTNERS:
        pl.semaphore_signal(barrier, inc=1, device_id=dev(*offset), device_id_type=MESH)
    pl.semaphore_wait(barrier, len(PARTNERS))

    load_g.wait()

    def slot(rep, xx, lo=0, n=DB):
        return G.at[rep, pl.ds(pl.multiple_of((l * 4 + xx) * DB + lo, 16), n), :]

    xm = lax.rem(x + 3, 4)
    xp = lax.rem(x + 1, 4)
    o = 1 - h
    RIGHT, LEFT, ACROSS, OTHER = (1, 0, 0, 0), (-1, 0, 0, 0), (0, 2, 0, 0), (0, 0, 0, 1)

    def own(lo, offset):
        return go(g_ref.at[pl.ds(lo, HB)], slot(h, x, lo, HB), offset)

    r0, l1, a0, a1, r1, l0 = own(0, RIGHT), own(HB, LEFT), own(0, ACROSS), own(HB, ACROSS), own(HB, RIGHT), own(0, LEFT)
    fo = pl.multiple_of((l * 8 + x * 2 + h) * FB, 128)
    own_w = pltpu.make_async_copy(
        w_ref.at[:, pl.ds(fo, FB)], Wb.at[pl.ds(pl.multiple_of((l * 4 + x) * DB, 16), DB), :], ls.at[0]
    )
    own_w.start()
    G[h, pl.ds(pl.multiple_of((l * 4 + x) * DB, 16), DB), :] = g_ref[...]

    load_a.wait()
    T[...] = a_ref[...].T.reshape(4, 2, HB, TB)
    act = go(T.at[:, o], AT.at[h, :, c], ACROSS)
    AT[h, :, c] = T[:, h]
    act_own = same(AT.at[h, :, c], OTHER)

    r0.wait_recv()
    r2 = same(slot(h, xm, 0, HB), RIGHT)
    l1.wait_recv()
    l2 = same(slot(h, xp, HB, HB), LEFT)
    a0.wait_recv()
    ar0 = same(slot(o, x, 0, HB), RIGHT)
    a1.wait_recv()
    al1 = same(slot(o, x, HB, HB), LEFT)
    ar1 = same(slot(o, x, HB, HB), RIGHT)
    al0 = same(slot(o, x, 0, HB), LEFT)
    for cp in (r1, l0, r2, l2):
        cp.wait_recv()
    own_row = G.at[h, pl.ds(pl.multiple_of(l * ROW, 16), ROW), :]
    row_up = same(own_row, (0, 1, 0, 0))
    row_down = same(own_row, (0, -1, 0, 0))
    ar0.wait_recv()
    ar2 = same(slot(o, xm, 0, HB), RIGHT)
    al1.wait_recv()
    al2 = same(slot(o, xp, HB, HB), LEFT)

    def units(p):
        return pl.ds(p * PART, PART)

    def send_weights(p, moves):
        copies = []
        for dx, dy, first, rows in moves:
            X = lax.rem(x + (dx + 4), 4)
            Y = lax.rem(y + (dy + 4), 4)
            col = pl.multiple_of((lax.rem(Y, 2) * 8 + X * 2 + Y // 2) * FB + p * PART, 128)
            there = pl.ds(pl.multiple_of((l * 4 + x) * DB + first, 16), rows)
            copies.append(go(w_ref.at[pl.ds(first, rows), pl.ds(col, PART)], Wb.at[there, units(p)], (dx, dy, 0, 0)))
        return copies

    near = [send_weights(p, NEAR) for p in range(N_PARTS)]
    far = [send_weights(p, FAR) for p in (0, 1, 2)]

    act.wait_recv()
    act_other = same(AT.at[o, :, c], OTHER)
    act_own.wait_recv()
    act_other.wait_recv()
    for cp in (ar1, al0, ar2, al2):
        cp.wait_recv()

    def tile(zz, ll, n):
        rows = pl.ds(pl.multiple_of(ll * ROW + n * TILE, 16), TILE)
        acc = lax.dot_general(AT[0, zz].reshape(2 * HB, TB), G[0, rows, :], NT, preferred_element_type=F32)
        acc += lax.dot_general(AT[1, zz].reshape(2 * HB, TB), G[1, rows, :], NT, preferred_element_type=F32)
        return acc

    def cols(n):
        return pl.ds(pl.multiple_of(n * TILE, 128), TILE)

    UP, DOWN = (0, 0, 1, 0), (0, 0, -1, 0)
    zp = lax.rem(z + 1, 4)
    zm = lax.rem(z + 3, 4)
    zo = lax.rem(z + 2, 4)

    def chunk_parts(j):
        ll = l if j == 0 else 1 - l

        @pl.loop(0, ROW // TILE)
        def _(n):
            SB[j, 0, :, :, cols(n)] = tile(zo, ll, n).reshape(2, HB, TILE).astype(BF)

        up = go(SB.at[j, 0, 0], FW.at[j, 0], UP)
        down = go(SB.at[j, 0, 1], FW.at[j, 1], DOWN)

        @pl.loop(0, ROW // TILE)
        def _(n):
            part = tile(zp, ll, n).reshape(2, HB, TILE)
            SB[j, 1, 1, :, cols(n)] = part[1].astype(BF)
            H[j, 0, :, cols(n)] = part[0]

        c0 = go(SB.at[j, 1, 1], RV.at[j, 0, 1], UP)

        @pl.loop(0, ROW // TILE)
        def _(n):
            part = tile(zm, ll, n).reshape(2, HB, TILE)
            SB[j, 2, 0, :, cols(n)] = part[0].astype(BF)
            H[j, 1, :, cols(n)] = part[1]

        c1 = go(SB.at[j, 2, 0], RV.at[j, 1, 0], DOWN)
        return up, down, c0, c1

    def chunk_sums(j, copies):
        up, down, c0, c1 = copies
        up.wait_recv()
        SB[j, 1, 0] = (H[j, 0] + FW[j, 0].astype(F32)).astype(BF)
        c2 = go(SB.at[j, 1, 0], RV.at[j, 0, 0], UP)
        down.wait_recv()
        SB[j, 2, 1] = (H[j, 1] + FW[j, 1].astype(F32)).astype(BF)
        c3 = go(SB.at[j, 2, 1], RV.at[j, 1, 1], DOWN)
        return c0, c1, c2, c3

    def chunk_own(j):
        ll = l if j == 0 else 1 - l

        @pl.loop(0, ROW // TILE)
        def _(n):
            OWN[j, :, :, cols(n)] = tile(z, ll, n).reshape(2, HB, TILE)

    def chunk_end(j, copies):
        for cp in copies:
            cp.wait_recv()
        XS[j] = (OWN[j, 1 - c] + RV[j, 0, 1 - c].astype(F32) + RV[j, 1, 1 - c].astype(F32)).astype(BF)
        swap = go(XS.at[j], XR.at[j], OTHER)
        OWN[j, c] = OWN[j, c] + RV[j, 0, c].astype(F32) + RV[j, 1, c].astype(F32)
        return swap

    def chunk_out(j, swap):
        ll = l if j == 0 else 1 - l
        swap.wait_recv()
        mine = OWN[j, c]
        other = XR[j].astype(F32)
        even = jnp.where(c == 0, mine, other)
        odd = jnp.where(c == 0, other, mine)
        pieces = []
        for xx in range(4):
            pieces += [even[:, xx * DB:(xx + 1) * DB], odd[:, xx * DB:(xx + 1) * DB]]
        wg_ref[:, pl.ds(pl.multiple_of(ll * 2 * ROW, 128), 2 * ROW)] = jnp.concatenate(pieces, axis=1)

    def half_tokens(q):
        return pl.ds(pl.multiple_of(q * 256, 256), 256)

    def product(rep, ll, q):
        g = G[rep, pl.ds(pl.multiple_of(ll * ROW, 16), ROW), half_tokens(q)]
        return jnp.dot(Wt[...], g, preferred_element_type=F32)

    def turn(p, ll):
        @pl.loop(0, ROW // 384)
        def _(k):
            rows = pl.ds(pl.multiple_of(ll * ROW + k * 384, 16), 384)
            Wt[:, pl.ds(pl.multiple_of(k * 384, 128), 384)] = Wb[rows, units(p)].T

    def hidden_near(p):
        for cp in near[p]:
            cp.wait_recv()
        turn(p, l)

        @pl.loop(0, 2)
        def _(q):
            R[p, 0, :, half_tokens(q)] = product(0, l, q)
            R[p, 1, :, half_tokens(q)] = product(1, l, q)

    def hidden_far(p):
        for cp in far[p]:
            cp.wait_recv()
        ll = 1 - l
        turn(p, ll)

        @pl.loop(0, 2)
        def _(q):
            XB[p, :, half_tokens(q)] = (R[p, 1 - c, :, half_tokens(q)] + product(1 - c, ll, q)).astype(BF)

        half = go(XB.at[p], YB.at[p], OTHER)

        @pl.loop(0, 2)
        def _(q):
            R[p, c, :, half_tokens(q)] += product(c, ll, q)

        half.wait_recv()
        XF[p] = (R[p, c] + YB[p].astype(F32)).astype(BF)
        final = prepare(XF.at[p], hg_ref.at[pl.ds(p * PART, PART)], (0, 2, 0, 1))

        @pl.when(c != h)
        def _():
            final.start()

        @pl.when(c == h)
        def _():
            hg_ref[pl.ds(p * PART, PART), :] = XF[p]

        return final

    first = chunk_parts(0)
    chunk_own(0)
    first = chunk_sums(0, first)
    row_up.wait_recv()
    row_down.wait_recv()
    second = chunk_parts(1)
    chunk_own(1)
    own_w.wait()
    hidden_near(0)
    second = chunk_sums(1, second)
    hidden_near(1)
    hidden_near(2)
    swap0 = chunk_end(0, first)
    chunk_out(0, swap0)
    f0 = hidden_far(0)
    f1 = hidden_far(1)
    f2 = hidden_far(2)
    swap1 = chunk_end(1, second)
    chunk_out(1, swap1)

    @pl.when(c != h)
    def _():
        for cp in (f0, f1, f2):
            cp.wait()

    for cp in started:
        cp.wait_send()


def per_device(hidden_act, out_grad, down_weight):
    scratch = [
        pltpu.VMEM((TB, FB), BF),
        pltpu.VMEM((DB, TB), BF),
        pltpu.VMEM((2, 2 * ROW, TB), BF),
        pltpu.VMEM((2 * ROW, FB), BF),
        pltpu.VMEM((PART, ROW), BF),
        pltpu.VMEM((4, 2, HB, TB), BF),
        pltpu.VMEM((2, 4, 2, HB, TB), BF),
        pltpu.VMEM((2, 3, 2, HB, ROW), BF),
        pltpu.VMEM((2, 2, HB, ROW), BF),
        pltpu.VMEM((2, 2, 2, HB, ROW), BF),
        pltpu.VMEM((2, 2, HB, ROW), F32),
        pltpu.VMEM((2, 2, HB, ROW), F32),
        pltpu.VMEM((2, HB, ROW), BF),
        pltpu.VMEM((2, HB, ROW), BF),
        pltpu.VMEM((N_PARTS, PART, TB), BF),
        pltpu.VMEM((N_PARTS, PART, TB), BF),
        pltpu.VMEM((N_PARTS, PART, TB), BF),
        pltpu.VMEM((N_PARTS, 2, PART, TB), F32),
        pltpu.SemaphoreType.DMA((N_SEM,)),
        pltpu.SemaphoreType.DMA((N_SEM,)),
        pltpu.SemaphoreType.DMA((3,)),
    ]
    vmem = pl.BlockSpec(memory_space=pltpu.VMEM)
    held = pl.pallas_call(
        kernel,
        out_shape=(pltpu.VMEM((FB, TB), BF), pltpu.VMEM((HB, 16 * DB), F32)),
        in_specs=[pl.BlockSpec(memory_space=pl.ANY)] * 3,
        out_specs=(vmem, vmem),
        scratch_shapes=scratch,
        compiler_params=pltpu.CompilerParams(collective_id=0, has_side_effects=True, vmem_limit_bytes=63_000_000),
        cost_estimate=pl.CostEstimate(flops=10_900_000_000, bytes_accessed=20_000_000, transcendentals=0),
    )(hidden_act, out_grad.T, down_weight.T)
    return held


def solution(mesh):
    return jax.shard_map(
        per_device,
        mesh=mesh,
        in_specs=(P("dp", "tensor"), P("dp", "tensor"), P(None, "tensor")),
        out_specs=(P("tensor", "dp"), P(("tensor", "dp"), None)),
        check_vma=False,
    )
```

```python
import functools

import jax
import jax.numpy as jnp
from jax import lax
from jax.experimental import pallas as pl
from jax.experimental.pallas import tpu as pltpu
from jax.sharding import PartitionSpec as P

MESH = pl.DeviceIdType.MESH
BF = jnp.bfloat16
F32 = jnp.float32
DB = 288
HB = 144
TB = 512
FB = 1152
ROW = 4 * DB
PART = 384
N_PARTS = FB // PART
TILE = 384

NEAR = [(1, 0, 0, DB), (-1, 0, 0, DB), (2, 0, 0, DB)]
FAR = []
for _dx in (0, 1, -1, 2):
    FAR += [(_dx, 1, 0, HB), (_dx, -1, HB, HB)]
N_SEM = 80
PARTNERS = [(1, 0, 0, 0), (-1, 0, 0, 0), (2, 0, 0, 0), (0, 2, 0, 0), (0, 0, 1, 0), (0, 0, -1, 0), (0, 0, 0, 1), (0, 2, 0, 1)]
PARTNERS += [(dx, dy, 0, 0) for dx in (0, 1, -1, 2) for dy in (1, -1)]
NT = (((1,), (1,)), ((), ()))


def kernel(a_hbm, g_hbm, w_ref, hg_ref, wg_ref, a_ref, g_ref, G, Wb, Wt, T, AT, SB, FW, RV, H, OWN, XS, XR, XB, YB, XF, R, ss, rs, ls):
    t = lax.axis_index("tensor")
    r = lax.axis_index("dp")
    c = lax.rem(t, 2)
    x = lax.rem(t // 2, 4)
    l = t // 8
    h = lax.rem(r, 2)
    z = r // 2
    y = 2 * h + l

    def dev(dx, dy, dz, dc):
        X = lax.rem(x + (dx + 4), 4)
        Y = lax.rem(y + (dy + 4), 4)
        Z = lax.rem(z + (dz + 4), 4)
        C = lax.rem(c + dc, 2)
        return (Z * 2 + Y // 2, lax.rem(Y, 2) * 8 + X * 2 + C)

    count = [0]
    started = []

    def prepare(src, dst, offset):
        k = count[0]
        count[0] += 1
        return pltpu.make_async_remote_copy(
            src_ref=src, dst_ref=dst, send_sem=ss.at[k], recv_sem=rs.at[k], device_id=dev(*offset), device_id_type=MESH
        )

    def go(src, dst, offset):
        cp = prepare(src, dst, offset)
        cp.start()
        started.append(cp)
        return cp

    def same(ref, offset):
        return go(ref, ref, offset)

    load_g = pltpu.make_async_copy(g_hbm, g_ref, ls.at[1])
    load_g.start()
    load_a = pltpu.make_async_copy(a_hbm, a_ref, ls.at[2])
    load_a.start()
    barrier = pltpu.get_barrier_semaphore()
    for offset in PARTNERS:
        pl.semaphore_signal(barrier, inc=1, device_id=dev(*offset), device_id_type=MESH)
    pl.semaphore_wait(barrier, len(PARTNERS))

    load_g.wait()

    def slot(rep, xx, lo=0, n=DB):
        return G.at[rep, pl.ds(pl.multiple_of((l * 4 + xx) * DB + lo, 16), n), :]

    xm = lax.rem(x + 3, 4)
    xp = lax.rem(x + 1, 4)
    o = 1 - h
    RIGHT, LEFT, ACROSS, OTHER = (1, 0, 0, 0), (-1, 0, 0, 0), (0, 2, 0, 0), (0, 0, 0, 1)

    def own(lo, offset):
        return go(g_ref.at[pl.ds(lo, HB)], slot(h, x, lo, HB), offset)

    r0, l1, a0, a1, r1, l0 = own(0, RIGHT), own(HB, LEFT), own(0, ACROSS), own(HB, ACROSS), own(HB, RIGHT), own(0, LEFT)
    fo = pl.multiple_of((l * 8 + x * 2 + h) * FB, 128)
    own_w = pltpu.make_async_copy(
        w_ref.at[:, pl.ds(fo, FB)], Wb.at[pl.ds(pl.multiple_of((l * 4 + x) * DB, 16), DB), :], ls.at[0]
    )
    own_w.start()
    G[h, pl.ds(pl.multiple_of((l * 4 + x) * DB, 16), DB), :] = g_ref[...]

    load_a.wait()
    T[...] = a_ref[...].T.reshape(4, 2, HB, TB)
    AT[h, :, c] = T[:, h]
    act_own = same(AT.at[h, :, c], OTHER)

    r0.wait_recv()
    r2 = same(slot(h, xm, 0, HB), RIGHT)
    l1.wait_recv()
    l2 = same(slot(h, xp, HB, HB), LEFT)
    a0.wait_recv()
    act = go(T.at[:, o], AT.at[h, :, c], ACROSS)
    ar0 = same(slot(o, x, 0, HB), RIGHT)
    a1.wait_recv()
    al1 = same(slot(o, x, HB, HB), LEFT)
    ar1 = same(slot(o, x, HB, HB), RIGHT)
    al0 = same(slot(o, x, 0, HB), LEFT)
    for cp in (r1, l0, r2, l2):
        cp.wait_recv()
    own_row = G.at[h, pl.ds(pl.multiple_of(l * ROW, 16), ROW), :]
    row_up = same(own_row, (0, 1, 0, 0))
    row_down = same(own_row, (0, -1, 0, 0))
    ar0.wait_recv()
    ar2 = same(slot(o, xm, 0, HB), RIGHT)
    al1.wait_recv()
    al2 = same(slot(o, xp, HB, HB), LEFT)

    def units(p):
        return pl.ds(p * PART, PART)

    def send_weights(p, moves):
        copies = []
        for dx, dy, first, rows in moves:
            X = lax.rem(x + (dx + 4), 4)
            Y = lax.rem(y + (dy + 4), 4)
            col = pl.multiple_of((lax.rem(Y, 2) * 8 + X * 2 + Y // 2) * FB + p * PART, 128)
            there = pl.ds(pl.multiple_of((l * 4 + x) * DB + first, 16), rows)
            copies.append(go(w_ref.at[pl.ds(first, rows), pl.ds(col, PART)], Wb.at[there, units(p)], (dx, dy, 0, 0)))
        return copies

    near = [send_weights(p, NEAR) for p in range(N_PARTS)]
    far = [send_weights(p, FAR) for p in (0, 1, 2)]

    act.wait_recv()
    act_other = same(AT.at[o, :, c], OTHER)
    act_own.wait_recv()
    act_other.wait_recv()
    for cp in (ar1, al0, ar2, al2):
        cp.wait_recv()

    def tile(zz, ll, n):
        rows = pl.ds(pl.multiple_of(ll * ROW + n * TILE, 16), TILE)
        acc = lax.dot_general(AT[0, zz].reshape(2 * HB, TB), G[0, rows, :], NT, preferred_element_type=F32)
        acc += lax.dot_general(AT[1, zz].reshape(2 * HB, TB), G[1, rows, :], NT, preferred_element_type=F32)
        return acc

    def cols(n):
        return pl.ds(pl.multiple_of(n * TILE, 128), TILE)

    UP, DOWN = (0, 0, 1, 0), (0, 0, -1, 0)
    zp = lax.rem(z + 1, 4)
    zm = lax.rem(z + 3, 4)
    zo = lax.rem(z + 2, 4)

    def chunk_parts(j):
        ll = l if j == 0 else 1 - l

        @pl.loop(0, ROW // TILE)
        def _(n):
            SB[j, 0, :, :, cols(n)] = tile(zo, ll, n).reshape(2, HB, TILE).astype(BF)

        up = go(SB.at[j, 0, 0], FW.at[j, 0], UP)
        down = go(SB.at[j, 0, 1], FW.at[j, 1], DOWN)

        @pl.loop(0, ROW // TILE)
        def _(n):
            part = tile(zp, ll, n).reshape(2, HB, TILE)
            SB[j, 1, 1, :, cols(n)] = part[1].astype(BF)
            H[j, 0, :, cols(n)] = part[0]

        c0 = go(SB.at[j, 1, 1], RV.at[j, 0, 1], UP)

        @pl.loop(0, ROW // TILE)
        def _(n):
            part = tile(zm, ll, n).reshape(2, HB, TILE)
            SB[j, 2, 0, :, cols(n)] = part[0].astype(BF)
            H[j, 1, :, cols(n)] = part[1]

        c1 = go(SB.at[j, 2, 0], RV.at[j, 1, 0], DOWN)
        return up, down, c0, c1

    def chunk_sums(j, copies):
        up, down, c0, c1 = copies
        up.wait_recv()
        SB[j, 1, 0] = (H[j, 0] + FW[j, 0].astype(F32)).astype(BF)
        c2 = go(SB.at[j, 1, 0], RV.at[j, 0, 0], UP)
        down.wait_recv()
        SB[j, 2, 1] = (H[j, 1] + FW[j, 1].astype(F32)).astype(BF)
        c3 = go(SB.at[j, 2, 1], RV.at[j, 1, 1], DOWN)
        return c0, c1, c2, c3

    def chunk_own(j):
        ll = l if j == 0 else 1 - l

        @pl.loop(0, ROW // TILE)
        def _(n):
            OWN[j, :, :, cols(n)] = tile(z, ll, n).reshape(2, HB, TILE)

    def chunk_end(j, copies):
        for cp in copies:
            cp.wait_recv()
        XS[j] = (OWN[j, 1 - c] + RV[j, 0, 1 - c].astype(F32) + RV[j, 1, 1 - c].astype(F32)).astype(BF)
        swap = go(XS.at[j], XR.at[j], OTHER)
        OWN[j, c] = OWN[j, c] + RV[j, 0, c].astype(F32) + RV[j, 1, c].astype(F32)
        return swap

    def chunk_out(j, swap):
        ll = l if j == 0 else 1 - l
        swap.wait_recv()
        mine = OWN[j, c]
        other = XR[j].astype(F32)
        even = jnp.where(c == 0, mine, other)
        odd = jnp.where(c == 0, other, mine)
        pieces = []
        for xx in range(4):
            pieces += [even[:, xx * DB:(xx + 1) * DB], odd[:, xx * DB:(xx + 1) * DB]]
        wg_ref[:, pl.ds(pl.multiple_of(ll * 2 * ROW, 128), 2 * ROW)] = jnp.concatenate(pieces, axis=1)

    def half_tokens(q):
        return pl.ds(pl.multiple_of(q * 256, 256), 256)

    def product(rep, ll, q):
        g = G[rep, pl.ds(pl.multiple_of(ll * ROW, 16), ROW), half_tokens(q)]
        return jnp.dot(Wt[...], g, preferred_element_type=F32)

    def turn(p, ll):
        @pl.loop(0, ROW // 384)
        def _(k):
            rows = pl.ds(pl.multiple_of(ll * ROW + k * 384, 16), 384)
            Wt[:, pl.ds(pl.multiple_of(k * 384, 128), 384)] = Wb[rows, units(p)].T

    def hidden_near(p):
        for cp in near[p]:
            cp.wait_recv()
        turn(p, l)

        @pl.loop(0, 2)
        def _(q):
            R[p, 0, :, half_tokens(q)] = product(0, l, q)
            R[p, 1, :, half_tokens(q)] = product(1, l, q)

    def hidden_far(p):
        for cp in far[p]:
            cp.wait_recv()
        ll = 1 - l
        turn(p, ll)

        @pl.loop(0, 2)
        def _(q):
            XB[p, :, half_tokens(q)] = (R[p, 1 - c, :, half_tokens(q)] + product(1 - c, ll, q)).astype(BF)

        half = go(XB.at[p], YB.at[p], OTHER)

        @pl.loop(0, 2)
        def _(q):
            R[p, c, :, half_tokens(q)] += product(c, ll, q)

        half.wait_recv()
        XF[p] = (R[p, c] + YB[p].astype(F32)).astype(BF)
        final = prepare(XF.at[p], hg_ref.at[pl.ds(p * PART, PART)], (0, 2, 0, 1))

        @pl.when(c != h)
        def _():
            final.start()

        @pl.when(c == h)
        def _():
            hg_ref[pl.ds(p * PART, PART), :] = XF[p]

        return final

    first = chunk_parts(0)
    chunk_own(0)
    first = chunk_sums(0, first)
    row_up.wait_recv()
    row_down.wait_recv()
    second = chunk_parts(1)
    chunk_own(1)
    own_w.wait()
    hidden_near(0)
    second = chunk_sums(1, second)
    hidden_near(1)
    hidden_near(2)
    swap0 = chunk_end(0, first)
    chunk_out(0, swap0)
    f0 = hidden_far(0)
    f1 = hidden_far(1)
    f2 = hidden_far(2)
    swap1 = chunk_end(1, second)
    chunk_out(1, swap1)

    @pl.when(c != h)
    def _():
        for cp in (f0, f1, f2):
            cp.wait()

    for cp in started:
        cp.wait_send()


def per_device(hidden_act, out_grad, down_weight):
    scratch = [
        pltpu.VMEM((TB, FB), BF),
        pltpu.VMEM((DB, TB), BF),
        pltpu.VMEM((2, 2 * ROW, TB), BF),
        pltpu.VMEM((2 * ROW, FB), BF),
        pltpu.VMEM((PART, ROW), BF),
        pltpu.VMEM((4, 2, HB, TB), BF),
        pltpu.VMEM((2, 4, 2, HB, TB), BF),
        pltpu.VMEM((2, 3, 2, HB, ROW), BF),
        pltpu.VMEM((2, 2, HB, ROW), BF),
        pltpu.VMEM((2, 2, 2, HB, ROW), BF),
        pltpu.VMEM((2, 2, HB, ROW), F32),
        pltpu.VMEM((2, 2, HB, ROW), F32),
        pltpu.VMEM((2, HB, ROW), BF),
        pltpu.VMEM((2, HB, ROW), BF),
        pltpu.VMEM((N_PARTS, PART, TB), BF),
        pltpu.VMEM((N_PARTS, PART, TB), BF),
        pltpu.VMEM((N_PARTS, PART, TB), BF),
        pltpu.VMEM((N_PARTS, 2, PART, TB), F32),
        pltpu.SemaphoreType.DMA((N_SEM,)),
        pltpu.SemaphoreType.DMA((N_SEM,)),
        pltpu.SemaphoreType.DMA((3,)),
    ]
    vmem = pl.BlockSpec(memory_space=pltpu.VMEM)
    held = pl.pallas_call(
        kernel,
        out_shape=(pltpu.VMEM((FB, TB), BF), pltpu.VMEM((HB, 16 * DB), F32)),
        in_specs=[pl.BlockSpec(memory_space=pl.ANY)] * 3,
        out_specs=(vmem, vmem),
        scratch_shapes=scratch,
        compiler_params=pltpu.CompilerParams(collective_id=0, has_side_effects=True, vmem_limit_bytes=63_000_000),
        cost_estimate=pl.CostEstimate(flops=10_900_000_000, bytes_accessed=20_000_000, transcendentals=0),
    )(hidden_act, out_grad.T, down_weight.T)
    return held


def solution(mesh):
    return jax.shard_map(
        per_device,
        mesh=mesh,
        in_specs=(P("dp", "tensor"), P("dp", "tensor"), P(None, "tensor")),
        out_specs=(P("tensor", "dp"), P(("tensor", "dp"), None)),
        check_vma=False,
    )
```
